256 devices in a mesh: band: 8 (over y, x_lo), grow: 32 (over x_hi, z, core).
Axes of the slice: x: 4 (x_hi: 2, x_lo: 2; x = x_hi * 2 + x_lo), y: 4, z: 8, core: 2. Of those that a mesh axis runs over, the one named last changes fastest.
Arguments:
- pair_matrices: bfloat16 [16, 64, 15360], P(None, 'band', 'grow')
- screened: bfloat16 [15360, 15360], P('grow', 'band'), as said below
Outputs:
- sigma: float32 [16, 16], replicated
Inputs may be any that keep to these rules, and one draw needn't show every extreme that they name: screened is symmetric.
All inputs are finite; a program needn't handle non-finite values.
Results may differ from the reference program's by a relative error of at most 0.0003.
Values may be sent and summed in bfloat16 or wider, within the bound.
A program may use at most 192 MiB of HBM per device.

```python
import math
import jax
import jax.numpy as jnp
from jax import lax

NG = 15360
STATES = 16
BANDS = 64


def draw_pair_matrices(key, part):
    key = jax.random.fold_in(key, 11)
    common_key, single_key = jax.random.split(key)
    factor = 1.0 / math.sqrt(BANDS * NG)
    common = jax.random.normal(common_key, (BANDS, NG), jnp.float32)
    individual = jax.random.normal(single_key, (STATES, BANDS, NG), jnp.float32)
    pairs = (0.7 * common[None, :, :] + individual) * factor
    return pairs.astype(jnp.bfloat16)


def draw_screened(key, part):
    key = jax.random.fold_in(key, 7)
    random_key, diag_key = jax.random.split(key)
    random_part = jax.random.normal(random_key, (NG, NG), jnp.float32)
    diagonal = jnp.exp(jax.random.uniform(diag_key, (NG,), jnp.float32, 0.0, math.log(4.0)))
    symmetric = random_part + random_part.T
    matrix = symmetric + jnp.eye(NG, dtype=jnp.float32) * diagonal[None, :]
    return matrix.astype(jnp.bfloat16)


def setup_inputs(seed: int = 0) -> dict:
    arg_keys = jax.random.split(jax.random.key(seed), 3)
    pair_matrices = draw_pair_matrices(jax.random.fold_in(arg_keys[2], 71), 0)
    screened = draw_screened(jax.random.fold_in(arg_keys[2], 71), 0)
    return dict(pair_matrices=pair_matrices, screened=screened)


def reference(pair_matrices, screened):
    flat_pairs = pair_matrices.astype(jnp.float32).reshape(STATES * BANDS, NG)
    screened_pairs = jnp.dot(flat_pairs, screened.astype(jnp.float32), precision=lax.Precision.HIGHEST, preferred_element_type=jnp.float32)
    screened_pairs = screened_pairs.reshape(STATES, BANDS, NG)
    sigma = jnp.einsum("sbh,tbh->st", screened_pairs, pair_matrices.astype(jnp.float32), precision=lax.Precision.HIGHEST)
    return -sigma
```

```python
import functools

import jax
import jax.numpy as jnp
from jax import lax
from jax.experimental import pallas as pl
from jax.experimental.pallas import tpu as pltpu
from jax.sharding import PartitionSpec as P

MESH = pl.DeviceIdType.MESH


def half_of(a, b):
    odd = (a + b) % 2
    return jnp.where(odd == 1, a % 2, jnp.where(a > b, 1, 0))


def kernel(nb, m_hbm, w_hbm, out_ref, m_own, mt_own, w, rows, cols, gram, red1, red2,
           load_sem, row_send, row_recv, col_send, col_recv, fwd_send, red1_send, red1_recv, red2_send, red2_recv):
    p, q = lax.axis_index("band"), lax.axis_index("grow")
    core, chip = q % 2, q // 2
    line, side = chip // 2, chip % 2
    diag = line == p
    first = jnp.where(diag, side, half_of(line, p))
    n_rows, n_cols = m_own.shape
    n_chips = 2 * nb
    tile = mt_own.shape[0]

    load_m = pltpu.make_async_copy(m_hbm, m_own, load_sem.at[0])
    load_w = pltpu.make_async_copy(w_hbm, w, load_sem.at[1])
    load_m.start()
    load_w.start()

    def row_needed(p_to, chip_at, p_from):
        at = chip_at // 2
        return jnp.logical_or(at == p_to, half_of(at, p_to) == p_from % 2)

    def col_needed(p_at, chip_at, p_from, r):
        at = chip_at // 2
        here = chip_at % 2
        return jnp.where(at == p_at, jnp.logical_or(r // 2 == here, p_from % 2 == here), half_of(at, p_at) == p_from % 2)

    barrier = pltpu.get_barrier_semaphore()

    def greet(p_to, q_to):
        pl.semaphore_signal(barrier, inc=1, device_id=(p_to, q_to), device_id_type=MESH)

    def greet_columns(i, carry):
        p_from, r = i // 2, 2 * (i % 2) + core
        q_from = 4 * p + r

        @pl.when(jnp.logical_and(col_needed(p, chip, p_from, r), jnp.logical_or(p_from != p, q_from != q)))
        def _():
            greet(p_from, q_from)

        return carry

    lax.fori_loop(0, 2 * nb, greet_columns, 0)

    def greet_plane(i, carry):
        other = (2 * p + core + i) % (2 * nb)
        greet(other // 2, 2 * chip + other % 2)
        return carry

    lax.fori_loop(1, 2 * nb, greet_plane, 0)

    def greet_line(i, carry):
        greet(p, 2 * ((chip + i) % n_chips) + core)
        return carry

    lax.fori_loop(1, n_chips, greet_line, 0)

    load_m.wait()
    mt_own[...] = m_own[...].T

    def sends_column(chip_to):
        needed = col_needed(line, chip_to, p, q % 4)
        return jnp.logical_and(needed, jnp.logical_or(p != line, chip_to != chip))

    def count(i, total):
        return total + jnp.where(sends_column(i), 1, 0)

    n_columns = lax.fori_loop(0, n_chips, count, 0)
    pl.semaphore_wait(barrier, n_columns + (2 * nb - 1) + (n_chips - 1))

    def column_copy(chip_to):
        return pltpu.make_async_remote_copy(
            src_ref=mt_own, dst_ref=cols.at[p, q % 4], send_sem=col_send.at[chip_to], recv_sem=col_recv.at[p, q % 4],
            device_id=(line, 2 * chip_to + core), device_id_type=MESH)

    def row_copy(p_to):
        return pltpu.make_async_remote_copy(
            src_ref=m_own, dst_ref=rows.at[p], send_sem=row_send.at[p_to], recv_sem=row_recv.at[p],
            device_id=(p_to, q), device_id_type=MESH)

    def send_columns(i, carry):
        chip_to = (chip + i) % n_chips

        @pl.when(sends_column(chip_to))
        def _():
            column_copy(chip_to).start()

        return carry

    lax.fori_loop(0, n_chips, send_columns, 0)

    def sends_row(p_to):
        return jnp.logical_and(p_to != p, row_needed(p_to, chip, p))

    def send_rows(i, carry):
        p_to = (p + i) % nb

        @pl.when(sends_row(p_to))
        def _():
            row_copy(p_to).start()

        return carry

    lax.fori_loop(1, nb, send_rows, 0)

    rows[p] = m_own[...]
    load_w.wait()

    @pl.when(diag)
    def _():
        cols[p, q % 4] = mt_own[...]
        lane = lax.broadcasted_iota(jnp.int32, w.shape, 1)
        own_half = (lane >= side * 2 * tile) & (lane < (side + 1) * 2 * tile)
        w[...] = jnp.where(own_half, w[...] * jnp.bfloat16(0.5), w[...])

        def clear(k, carry):
            p_from = 2 * k + 1 - side
            for r in range(2):
                cols[p_from, 2 * (1 - side) + r] = jnp.zeros((tile, n_rows), jnp.bfloat16)
            return carry

        lax.fori_loop(0, nb // 2, clear, 0)

    gram[...] = jnp.zeros_like(gram)

    def forward(p_from, r):
        return pltpu.make_async_remote_copy(
            src_ref=cols.at[p_from, r], dst_ref=cols.at[p_from, r], send_sem=fwd_send.at[p_from, r],
            recv_sem=col_recv.at[p_from, r], device_id=(p, q + 1 - 2 * core), device_id_type=MESH)

    group = min(2, nb // 2)
    steps = (nb // 2) // group
    n_steps = jnp.where(diag, 2 * steps, steps)

    def band_of(step, j):
        half = jnp.where(step < steps, first, 1 - first)
        return 2 * ((step % steps) * group + j) + half

    def step_body(step, carry):
        for j in range(group):
            p_from = band_of(step, j)
            for k in range(2):
                r = 2 * k + core

                @pl.when(col_needed(p, chip, p_from, r))
                def _():
                    @pl.when(jnp.logical_or(p_from != p, 4 * p + r != q))
                    def _():
                        forward(p_from, r).wait_recv()

                    forward(p_from, r).start()

        for j in range(group):
            p_from = band_of(step, j)
            for k in range(2):
                r = 2 * k + 1 - core

                @pl.when(col_needed(p, chip, p_from, r))
                def _():
                    forward(p_from, r).wait_recv()

            @pl.when(p_from != p)
            def _():
                pltpu.make_async_remote_copy(
                    src_ref=m_own, dst_ref=rows.at[p_from], send_sem=row_send.at[p_from], recv_sem=row_recv.at[p_from],
                    device_id=(p_from, q), device_id_type=MESH).wait_recv()

        right = [cols[band_of(step, j)].reshape(4 * tile, n_rows) for j in range(group)]
        z = jnp.dot(w[...], jnp.concatenate(right, axis=1), preferred_element_type=jnp.float32)
        high = z.astype(jnp.bfloat16)
        low = (z - high.astype(jnp.float32)).astype(jnp.bfloat16)
        for j in range(group):
            part = slice(j * n_rows, (j + 1) * n_rows)
            both = jnp.concatenate([high[:, part], low[:, part]], axis=1)
            g = jnp.dot(rows[band_of(step, j)], both, preferred_element_type=jnp.float32)
            gram[...] += g[:, :n_rows] + g[:, n_rows:]
        return carry

    lax.fori_loop(0, n_steps, step_body, 0)

    bands = n_rows // 16
    row_id = lax.broadcasted_iota(jnp.int32, gram.shape, 0)
    lane_id = lax.broadcasted_iota(jnp.int32, gram.shape, 1)
    kept = jnp.where(row_id % bands == lane_id % bands, gram[...], 0.0)
    place1 = 2 * p + core
    red1[place1] = kept.reshape(16, bands, n_rows).sum(axis=1)

    def plane_copy(other):
        return pltpu.make_async_remote_copy(
            src_ref=red1.at[place1], dst_ref=red1.at[place1], send_sem=red1_send.at[other], recv_sem=red1_recv.at[place1],
            device_id=(other // 2, 2 * chip + other % 2), device_id_type=MESH)

    def plane_wait(other):
        pltpu.make_async_remote_copy(
            src_ref=red1.at[place1], dst_ref=red1.at[other], send_sem=red1_send.at[other], recv_sem=red1_recv.at[other],
            device_id=(other // 2, 2 * chip + other % 2), device_id_type=MESH).wait_recv()

    def line_copy(other):
        return pltpu.make_async_remote_copy(
            src_ref=red2.at[chip], dst_ref=red2.at[chip], send_sem=red2_send.at[other], recv_sem=red2_recv.at[chip],
            device_id=(p, 2 * other + core), device_id_type=MESH)

    def line_wait(other):
        pltpu.make_async_remote_copy(
            src_ref=red2.at[chip], dst_ref=red2.at[other], send_sem=red2_send.at[other], recv_sem=red2_recv.at[other],
            device_id=(p, 2 * other + core), device_id_type=MESH).wait_recv()

    def loop(lo, hi, act):
        def body(i, carry):
            act(i)
            return carry

        lax.fori_loop(lo, hi, body, 0)

    loop(1, 2 * nb, lambda i: plane_copy((place1 + i) % (2 * nb)).start())
    loop(1, 2 * nb, lambda i: plane_wait((place1 + i) % (2 * nb)))
    red2[chip] = red1[...].sum(axis=0)
    loop(1, n_chips, lambda i: line_copy((chip + i) % n_chips).start())
    loop(1, n_chips, lambda i: line_wait((chip + i) % n_chips))
    total = red2[...].sum(axis=0)
    fold = jnp.where(
        lax.broadcasted_iota(jnp.int32, (n_rows, 16), 0) // bands == lax.broadcasted_iota(jnp.int32, (n_rows, 16), 1), 1.0, 0.0)
    s = jnp.dot(total, fold, precision=lax.Precision.HIGHEST, preferred_element_type=jnp.float32)
    s_t = lax.dot_general(fold, total, (((0,), (1,)), ((), ())), precision=lax.Precision.HIGHEST,
                          preferred_element_type=jnp.float32)
    out_ref[...] = -(s + s_t)

    loop(1, 2 * nb, lambda i: plane_copy((place1 + i) % (2 * nb)).wait_send())
    loop(1, n_chips, lambda i: line_copy((chip + i) % n_chips).wait_send())

    def sent_column(i):
        @pl.when(sends_column(i))
        def _():
            column_copy(i).wait_send()

    def sent_row(i):
        @pl.when(sends_row(i))
        def _():
            row_copy(i).wait_send()

    def sent_forward(i):
        p_from, r = i // 2, 2 * (i % 2) + core

        @pl.when(col_needed(p, chip, p_from, r))
        def _():
            forward(p_from, r).wait_send()

    loop(0, n_chips, sent_column)
    loop(0, nb, sent_row)
    loop(0, 2 * nb, sent_forward)


def body(nb, pair_matrices, screened):
    states, bands, tile = pair_matrices.shape
    flat = pair_matrices.reshape(states * bands, tile)
    n = states * bands
    dma = pltpu.SemaphoreType.DMA
    return pl.pallas_call(
        functools.partial(kernel, nb),
        out_shape=jax.ShapeDtypeStruct((states, states), jnp.float32),
        in_specs=[pl.BlockSpec(memory_space=pl.ANY)] * 2,
        out_specs=pl.BlockSpec(memory_space=pltpu.VMEM),
        scratch_shapes=[
            pltpu.VMEM((n, tile), jnp.bfloat16),
            pltpu.VMEM((tile, n), jnp.bfloat16),
            pltpu.VMEM(screened.shape, jnp.bfloat16),
            pltpu.VMEM((nb, n, tile), jnp.bfloat16),
            pltpu.VMEM((nb, 4, tile, n), jnp.bfloat16),
            pltpu.VMEM((n, n), jnp.float32),
            pltpu.VMEM((2 * nb, states, n), jnp.float32),
            pltpu.VMEM((2 * nb, states, n), jnp.float32),
            dma((2,)), dma((nb,)), dma((nb,)), dma((2 * nb,)), dma((nb, 4)), dma((nb, 4)),
            dma((2 * nb,)), dma((2 * nb,)), dma((2 * nb,)), dma((2 * nb,)),
        ],
        compiler_params=pltpu.CompilerParams(collective_id=0, has_side_effects=True, vmem_limit_bytes=40 * 1024 * 1024),
    )(flat, screened)


def solution(mesh):
    placed = (P(None, "band", "grow"), P("grow", "band"))
    return jax.shard_map(functools.partial(body, mesh.shape["band"]), mesh=mesh, in_specs=placed, out_specs=P(), check_vma=False)
```

```python
import functools

import jax
import jax.numpy as jnp
from jax import lax
from jax.experimental import pallas as pl
from jax.experimental.pallas import tpu as pltpu
from jax.sharding import PartitionSpec as P

MESH = pl.DeviceIdType.MESH

SHARES = {
    8: [
        [0, 170, 27, 154, 120, 116, 177, 101],
        [85, 0, 85, 114, 57, 177, 170, 166],
        [228, 170, 0, 170, 198, 85, 106, 89],
        [101, 141, 85, 0, 154, 216, 226, 83],
        [135, 198, 57, 101, 0, 170, 27, 154],
        [139, 78, 170, 39, 85, 0, 85, 114],
        [78, 85, 149, 29, 228, 170, 0, 170],
        [154, 89, 166, 172, 101, 141, 85, 0],
    ],
    4: [[0, 3, 5, 9], [12, 0, 6, 10], [10, 9, 0, 3], [6, 5, 12, 0]],
}


def pick(index, values):
    out = jnp.int32(values[0])
    for i, v in enumerate(values[1:], 1):
        out = jnp.where(index == i, jnp.int32(v), out)
    return out


def bit(mask, i):
    return (mask >> i) & 1 == 1


def loop(lo, hi, act):
    def body(i, carry):
        act(i)
        return carry

    lax.fori_loop(lo, hi, body, 0)


def kernel(nb, m_hbm, w_hbm, out_ref, m_own, mt_own, w, rows, cols, gram, red1, red2,
           load_sem, w_sem, plane_send, rows_recv, rows_fwd, cols_recv, cols_send, column_send,
           red1_send, red1_recv, red2_send, red2_recv):
    share = SHARES[nb]
    zs, pairs = nb, nb // 2
    full = (1 << nb) - 1
    even = sum(1 << i for i in range(0, nb, 2))
    p, q = lax.axis_index("band"), lax.axis_index("grow")
    core, chip = q % 2, q // 2
    pair, side = chip // 2, chip % 2
    diag = pair == p
    tile, n = mt_own.shape
    window = w.shape[1]
    pad = window - 2 * tile
    sibling = (p, q + 1 - 2 * core)

    def chip_at(line, chip_to, core_at):
        return (line, 2 * chip_to + core_at)

    beside = chip + 1 - 2 * side

    load_m = pltpu.make_async_copy(m_hbm, m_own, load_sem.at[0])
    load_m.start()
    own_rows = pl.ds(pl.multiple_of(core * tile, 16), tile)
    far = 4 * tile - window
    load_w = pltpu.make_async_copy(w_hbm.at[:, pl.ds(pl.multiple_of(core * far, 128), window)], w.at[own_rows], load_sem.at[1])
    load_w.start()
    give_w = pltpu.make_async_remote_copy(
        src_ref=w_hbm.at[:, pl.ds(pl.multiple_of((1 - core) * far, 128), window)], dst_ref=w.at[own_rows],
        send_sem=w_sem.at[0], recv_sem=w_sem.at[1], device_id=sibling, device_id_type=MESH)

    barrier = pltpu.get_barrier_semaphore()

    def greet(device):
        pl.semaphore_signal(barrier, inc=1, device_id=device, device_id_type=MESH)

    place1 = 2 * p + core

    def plane_device(i):
        return (i // 2, 2 * chip + i % 2)

    loop(1, 2 * nb, lambda i: greet(plane_device((place1 + i) % (2 * nb))))
    loop(1, 2 * zs, lambda i: greet(chip_at(p, (chip + i) % (2 * zs), core)))

    def words_of(line):
        words = []
        for r in range(2):
            v = [sum(share[r * pairs + i][l] << (nb * i) for i in range(pairs)) for l in range(nb)]
            words.append(pick(line, [x - (x >> 31 << 32) for x in v]))
        return words

    def shared(at, words):
        return (jnp.where(at // pairs == 0, words[0], words[1]) >> (nb * (at % pairs))) & full

    def leader(at, line, c):
        return pick((at + pairs - line % pairs) % pairs, [c, 0] if pairs == 2 else [c, 0, 1 - c, 1])

    def straight(at, line, c):
        ahead = (at + pairs - line % pairs) % pairs
        return ((ahead == 1) & (c == 1)) | ((ahead == pairs - 1) & (c == 0))

    def targets(line, words, c, pp, act):
        def one(i):
            at = (line + 1 + i) % nb
            home = at == line
            goes = jnp.where(home, pp % 2 == 1 - c, bit(shared(at, words), pp))
            to = 2 * at + jnp.where(home, 1 - c, leader(at, line, c))

            @pl.when(goes)
            def _():
                act(0, at, to)

            @pl.when(goes & ~home & straight(at, line, c))
            def _():
                act(1, at, 2 * at + 1 - leader(at, line, c))

        loop(0, nb, one)

    own_words = words_of(p)
    here = jnp.where(~diag, shared(pair, own_words), jnp.where(side == core, 0, jnp.where(side == 0, even, full - even)))
    direct = diag | straight(pair, p, core) | (side == leader(pair, p, core))
    leads = direct & ~diag & ~straight(pair, p, core)
    row_mask = jnp.where(diag, 0, shared(pair, own_words))
    to_lines = jnp.int32(0)
    for l in range(nb):
        m = pick(pair, [share[r][l] for r in range(nb)])
        to_lines |= jnp.where((m >> p) & 1 == 1, 1 << l, 0)
    def greet_sender(pp):
        @pl.when(direct & bit(here, pp))
        def _():
            for j in range(2):
                greet((pp, 2 * (2 * p + core) + j))

    loop(0, nb, greet_sender)
    load_m.wait()
    mt_own[...] = m_own[...].T
    shard_words = words_of(pair)

    def count(i, total):
        at = (pair + i) % nb
        one = bit(shared(at, shard_words), p)
        return total + jnp.where(one, jnp.where(straight(at, pair, side), 2, 1), 0)

    n_columns = lax.fori_loop(1, nb, count, jnp.where(p % 2 == 1 - side, 1, 0))
    pl.semaphore_wait(barrier, 4 * nb - 2 + n_columns)
    give_w.start()

    def col_place(pp, c, j):
        return cols.at[pp, pl.ds(pl.multiple_of(pad * c + tile * j, 16), tile)]

    def column_copy(k, at, to):
        return pltpu.make_async_remote_copy(
            src_ref=mt_own, dst_ref=col_place(p, side, core), send_sem=column_send.at[at, k], recv_sem=cols_recv.at[p, core],
            device_id=chip_at(pair, to, side), device_id_type=MESH)

    targets(pair, shard_words, side, p, lambda k, at, to: column_copy(k, at, to).start())

    keeps = diag & (core == side)
    to_diag = pltpu.make_async_remote_copy(
        src_ref=mt_own, dst_ref=col_place(p, side, core), send_sem=plane_send.at[nb], recv_sem=cols_recv.at[p, core],
        device_id=(pair, 2 * chip + side), device_id_type=MESH)

    @pl.when(~keeps)
    def _():
        to_diag.start()

    def row_copy(line):
        return pltpu.make_async_remote_copy(
            src_ref=m_own, dst_ref=rows.at[p, core], send_sem=plane_send.at[line], recv_sem=rows_recv.at[p, core],
            device_id=(line, q), device_id_type=MESH)

    def sends_row(line):
        return bit(to_lines, line) & (line != p) & (line != pair)

    def send_row(i):
        line = (p + i) % nb

        @pl.when(sends_row(line))
        def _():
            row_copy(line).start()

    loop(1, nb, send_row)

    def row_forward(pp, j):
        return pltpu.make_async_remote_copy(
            src_ref=rows.at[pp, j], dst_ref=rows.at[pp, j], send_sem=rows_fwd.at[pp, j], recv_sem=rows_recv.at[pp, j],
            device_id=sibling, device_id_type=MESH)

    @pl.when(bit(row_mask, p))
    def _():
        rows[p, core] = m_own[...]

    @pl.when(keeps)
    def _():
        cols[p, pl.ds(pl.multiple_of(pad * side + tile * core, 16), tile)] = mt_own[...]

    if pad:
        def clear(pp):
            cols[pp, pl.ds(pl.multiple_of(2 * tile * (1 - core), 16), pad)] = jnp.zeros((pad, n), jnp.bfloat16)

        loop(0, nb, clear)
    gram[...] = jnp.zeros_like(gram)

    def share_row(pp):
        @pl.when(bit(row_mask, pp))
        def _():
            @pl.when(pp != p)
            def _():
                row_forward(pp, core).wait_recv()

            row_forward(pp, core).start()

    loop(0, nb, share_row)

    def col_copy(pp, j):
        place = col_place(pp, core, j)
        return pltpu.make_async_remote_copy(
            src_ref=place, dst_ref=place, send_sem=cols_send.at[pp, j], recv_sem=cols_recv.at[pp, j],
            device_id=chip_at(p, beside, core), device_id_type=MESH)

    def receive(pp):
        for j in range(2):
            @pl.when(~(keeps & (pp == p) & (j == core)))
            def _():
                col_copy(pp, j).wait_recv()

    def hand_on(pp):
        @pl.when(bit(here, pp))
        def _():
            receive(pp)
            for j in range(2):
                col_copy(pp, j).start()

    @pl.when(leads)
    def _():
        loop(0, nb, hand_on)

    give_w.wait_recv()
    load_w.wait()
    from_sibling = diag & (core != side)

    def use(pp):
        @pl.when(~leads)
        def _():
            receive(pp)

        @pl.when(keeps)
        def _():
            for j in range(2):
                part = cols[pp, pl.ds(pl.multiple_of(pad * side + tile * j, 16), tile)]
                rows[pp, j] = part.T

                @pl.when(pp % 2 == side)
                def _():
                    row_forward(pp, j).start()

        @pl.when(~keeps)
        def _():
            for j in range(2):
                @pl.when(from_sibling | (j != core))
                def _():
                    row_forward(pp, j).wait_recv()

        t = jnp.dot(w[...], cols[pp], preferred_element_type=jnp.float32)
        high = t.astype(jnp.bfloat16)
        low = (t - high.astype(jnp.float32)).astype(jnp.bfloat16)
        both = jnp.concatenate([high, low], axis=1)
        g = jnp.dot(rows[pp, 0], both[:tile], preferred_element_type=jnp.float32)
        g += jnp.dot(rows[pp, 1], both[tile:], preferred_element_type=jnp.float32)
        gram[...] += g[:, :n] + g[:, n:]

    def use_all(pp):
        @pl.when(keeps | bit(here, pp))
        def _():
            use(pp)

    loop(0, nb, use_all)

    bands = n // 16
    row_id = lax.broadcasted_iota(jnp.int32, gram.shape, 0)
    lane_id = lax.broadcasted_iota(jnp.int32, gram.shape, 1)
    kept = jnp.where(row_id % bands == lane_id % bands, gram[...], 0.0) * jnp.where(keeps, 0.5, 1.0)
    red1[place1] = kept.reshape(16, bands, n).sum(axis=1)

    def plane_copy(other):
        return pltpu.make_async_remote_copy(
            src_ref=red1.at[place1], dst_ref=red1.at[place1], send_sem=red1_send.at[other], recv_sem=red1_recv.at[place1],
            device_id=plane_device(other), device_id_type=MESH)

    def plane_wait(other):
        pltpu.make_async_remote_copy(
            src_ref=red1.at[place1], dst_ref=red1.at[other], send_sem=red1_send.at[other], recv_sem=red1_recv.at[other],
            device_id=plane_device(other), device_id_type=MESH).wait_recv()

    loop(1, 2 * nb, lambda i: plane_copy((place1 + i) % (2 * nb)).start())
    give_w.wait_send()
    targets(pair, shard_words, side, p, lambda k, at, to: column_copy(k, at, to).wait_send())

    @pl.when(~keeps)
    def _():
        to_diag.wait_send()

    def sent(pp):
        @pl.when((pp != p) & sends_row(pp))
        def _():
            row_copy(pp).wait_send()

        @pl.when(bit(row_mask, pp))
        def _():
            row_forward(pp, core).wait_send()

        for j in range(2):
            @pl.when(leads & bit(here, pp))
            def _():
                col_copy(pp, j).wait_send()

            @pl.when(keeps & (pp % 2 == side))
            def _():
                row_forward(pp, j).wait_send()

    loop(0, nb, sent)
    loop(1, 2 * nb, lambda i: plane_wait((place1 + i) % (2 * nb)))
    red2[chip] = red1[...].sum(axis=0)

    def line_copy(other):
        return pltpu.make_async_remote_copy(
            src_ref=red2.at[chip], dst_ref=red2.at[chip], send_sem=red2_send.at[other], recv_sem=red2_recv.at[chip],
            device_id=chip_at(p, other, core), device_id_type=MESH)

    def line_wait(other):
        pltpu.make_async_remote_copy(
            src_ref=red2.at[chip], dst_ref=red2.at[other], send_sem=red2_send.at[other], recv_sem=red2_recv.at[other],
            device_id=chip_at(p, other, core), device_id_type=MESH).wait_recv()

    loop(1, 2 * zs, lambda i: line_copy((chip + i) % (2 * zs)).start())
    loop(1, 2 * zs, lambda i: line_wait((chip + i) % (2 * zs)))
    total = red2[...].sum(axis=0)
    fold = jnp.where(
        lax.broadcasted_iota(jnp.int32, (n, 16), 0) // bands == lax.broadcasted_iota(jnp.int32, (n, 16), 1), 1.0, 0.0)
    s = jnp.dot(total, fold, precision=lax.Precision.HIGHEST, preferred_element_type=jnp.float32)
    s_t = lax.dot_general(fold, total, (((0,), (1,)), ((), ())), precision=lax.Precision.HIGHEST,
                          preferred_element_type=jnp.float32)
    out_ref[...] = -(s + s_t)

    loop(1, 2 * nb, lambda i: plane_copy((place1 + i) % (2 * nb)).wait_send())
    loop(1, 2 * zs, lambda i: line_copy((chip + i) % (2 * zs)).wait_send())


def body(nb, pair_matrices, screened):
    states, bands, tile = pair_matrices.shape
    n = states * bands
    flat = pair_matrices.reshape(n, tile)
    window = -(-2 * tile // 128) * 128
    dma = pltpu.SemaphoreType.DMA
    small = pltpu.VMEM((2 * nb, states, n), jnp.float32)
    return pl.pallas_call(
        functools.partial(kernel, nb),
        out_shape=jax.ShapeDtypeStruct((states, states), jnp.float32),
        in_specs=[pl.BlockSpec(memory_space=pl.ANY)] * 2,
        out_specs=pl.BlockSpec(memory_space=pltpu.VMEM),
        scratch_shapes=[
            pltpu.VMEM((n, tile), jnp.bfloat16),
            pltpu.VMEM((tile, n), jnp.bfloat16),
            pltpu.VMEM((2 * tile, window), jnp.bfloat16),
            pltpu.VMEM((nb, 2, n, tile), jnp.bfloat16),
            pltpu.VMEM((nb, window, n), jnp.bfloat16),
            pltpu.VMEM((n, n), jnp.float32),
            small,
            small,
            dma((2,)), dma((2,)), dma((nb + 1,)), dma((nb, 2)), dma((nb, 2)), dma((nb, 2)), dma((nb, 2)), dma((nb, 2)),
            dma((2 * nb,)), dma((2 * nb,)), dma((2 * nb,)), dma((2 * nb,)),
        ],
        compiler_params=pltpu.CompilerParams(collective_id=0, has_side_effects=True, vmem_limit_bytes=40 * 1024 * 1024),
    )(flat, screened)


def solution(mesh):
    placed = (P(None, "band", "grow"), P("grow", "band"))
    return jax.shard_map(functools.partial(body, mesh.shape["band"]), mesh=mesh, in_specs=placed, out_specs=P(), check_vma=False)
```

```python
import functools

import jax
import jax.numpy as jnp
from jax import lax
from jax.experimental import pallas as pl
from jax.experimental.pallas import tpu as pltpu
from jax.sharding import PartitionSpec as P

MESH = pl.DeviceIdType.MESH

SHARES = {
    8: [
        [0, 170, 27, 154, 120, 116, 177, 101],
        [85, 0, 85, 114, 57, 177, 170, 166],
        [228, 170, 0, 170, 198, 85, 106, 89],
        [101, 141, 85, 0, 154, 216, 226, 83],
        [135, 198, 57, 101, 0, 170, 27, 154],
        [139, 78, 170, 39, 85, 0, 85, 114],
        [78, 85, 149, 29, 228, 170, 0, 170],
        [154, 89, 166, 172, 101, 141, 85, 0],
    ],
    4: [[0, 3, 5, 9], [12, 0, 6, 10], [10, 9, 0, 3], [6, 5, 12, 0]],
}


def pick(index, values):
    out = jnp.int32(values[0])
    for i, v in enumerate(values[1:], 1):
        out = jnp.where(index == i, jnp.int32(v), out)
    return out


def bit(mask, i):
    return (mask >> i) & 1 == 1


def loop(lo, hi, act):
    def body(i, carry):
        act(i)
        return carry

    lax.fori_loop(lo, hi, body, 0)


def kernel(nb, m_hbm, w_hbm, out_ref, m_own, mt_own, w, rows, cols, gram, red1, red2,
           load_sem, w_sem, plane_send, rows_recv, rows_fwd, cols_recv, cols_send, column_send,
           red1_send, red1_recv, red2_send, red2_recv):
    share = SHARES[nb]
    zs, pairs = nb, nb // 2
    full = (1 << nb) - 1
    even = sum(1 << i for i in range(0, nb, 2))
    p, q = lax.axis_index("band"), lax.axis_index("grow")
    core, chip = q % 2, q // 2
    pair, side = chip // 2, chip % 2
    diag = pair == p
    tile, n = mt_own.shape
    window = w.shape[1]
    pad = window - 2 * tile
    sibling = (p, q + 1 - 2 * core)

    def chip_at(line, chip_to, core_at):
        return (line, 2 * chip_to + core_at)

    beside = chip + 1 - 2 * side

    load_m = pltpu.make_async_copy(m_hbm, m_own, load_sem.at[0])
    load_m.start()
    own_rows = pl.ds(pl.multiple_of(core * tile, 16), tile)
    far = 4 * tile - window
    load_w = pltpu.make_async_copy(w_hbm.at[:, pl.ds(pl.multiple_of(core * far, 128), window)], w.at[own_rows], load_sem.at[1])
    load_w.start()
    give_w = pltpu.make_async_remote_copy(
        src_ref=w_hbm.at[:, pl.ds(pl.multiple_of((1 - core) * far, 128), window)], dst_ref=w.at[own_rows],
        send_sem=w_sem.at[0], recv_sem=w_sem.at[1], device_id=sibling, device_id_type=MESH)

    barrier = pltpu.get_barrier_semaphore()

    def greet(device):
        pl.semaphore_signal(barrier, inc=1, device_id=device, device_id_type=MESH)

    place1 = 2 * p + core

    def plane_device(i):
        return (i // 2, 2 * chip + i % 2)

    loop(1, 2 * nb, lambda i: greet(plane_device((place1 + i) % (2 * nb))))
    loop(1, 2 * zs, lambda i: greet(chip_at(p, (chip + i) % (2 * zs), core)))

    def words_of(line):
        words = []
        for r in range(2):
            v = [sum(share[r * pairs + i][l] << (nb * i) for i in range(pairs)) for l in range(nb)]
            words.append(pick(line, [x - (x >> 31 << 32) for x in v]))
        return words

    def shared(at, words):
        return (jnp.where(at // pairs == 0, words[0], words[1]) >> (nb * (at % pairs))) & full

    def leader(at, line, c):
        return pick((at + pairs - line % pairs) % pairs, [c, 0] if pairs == 2 else [c, 0, 1 - c, 1])

    def straight(at, line, c):
        ahead = (at + pairs - line % pairs) % pairs
        return ((ahead == 1) & (c == 1)) | ((ahead == pairs - 1) & (c == 0))

    def targets(line, words, c, pp, act):
        def one(i):
            at = (line + 1 + i) % nb
            home = at == line
            goes = jnp.where(home, pp % 2 == 1 - c, bit(shared(at, words), pp))
            to = 2 * at + jnp.where(home, 1 - c, leader(at, line, c))

            both = straight(at, line, c)

            @pl.when(goes & (i < nb) & ~home & ~both)
            def _():
                act(0, at, to)

            @pl.when(goes & (i >= nb) & (home | both))
            def _():
                act(0, at, to)

            @pl.when(goes & (i >= nb) & ~home & both)
            def _():
                act(1, at, 2 * at + 1 - leader(at, line, c))

        loop(0, 2 * nb, one)

    own_words = words_of(p)
    here = jnp.where(~diag, shared(pair, own_words), jnp.where(side == core, 0, jnp.where(side == 0, even, full - even)))
    direct = diag | straight(pair, p, core) | (side == leader(pair, p, core))
    leads = direct & ~diag & ~straight(pair, p, core)
    row_mask = jnp.where(diag, 0, shared(pair, own_words))
    to_lines = jnp.int32(0)
    for l in range(nb):
        m = pick(pair, [share[r][l] for r in range(nb)])
        to_lines |= jnp.where((m >> p) & 1 == 1, 1 << l, 0)
    def greet_sender(pp):
        @pl.when(direct & bit(here, pp))
        def _():
            for j in range(2):
                greet((pp, 2 * (2 * p + core) + j))

    loop(0, nb, greet_sender)
    load_m.wait()
    mt_own[...] = m_own[...].T
    shard_words = words_of(pair)

    def count(i, total):
        at = (pair + i) % nb
        one = bit(shared(at, shard_words), p)
        return total + jnp.where(one, jnp.where(straight(at, pair, side), 2, 1), 0)

    n_columns = lax.fori_loop(1, nb, count, jnp.where(p % 2 == 1 - side, 1, 0))
    pl.semaphore_wait(barrier, 4 * nb - 2 + n_columns)
    give_w.start()

    def col_place(pp, c, j):
        return cols.at[pp, pl.ds(pl.multiple_of(pad * c + tile * j, 16), tile)]

    def column_copy(k, at, to):
        return pltpu.make_async_remote_copy(
            src_ref=mt_own, dst_ref=col_place(p, side, core), send_sem=column_send.at[at, k], recv_sem=cols_recv.at[p, core],
            device_id=chip_at(pair, to, side), device_id_type=MESH)

    targets(pair, shard_words, side, p, lambda k, at, to: column_copy(k, at, to).start())

    keeps = diag & (core == side)
    to_diag = pltpu.make_async_remote_copy(
        src_ref=mt_own, dst_ref=col_place(p, side, core), send_sem=plane_send.at[nb], recv_sem=cols_recv.at[p, core],
        device_id=(pair, 2 * chip + side), device_id_type=MESH)

    @pl.when(~keeps)
    def _():
        to_diag.start()

    def row_copy(line):
        return pltpu.make_async_remote_copy(
            src_ref=m_own, dst_ref=rows.at[p, core], send_sem=plane_send.at[line], recv_sem=rows_recv.at[p, core],
            device_id=(line, q), device_id_type=MESH)

    def sends_row(line):
        return bit(to_lines, line) & (line != p) & (line != pair)

    def send_row(i):
        line = (p + i) % nb

        @pl.when(sends_row(line))
        def _():
            row_copy(line).start()

    loop(1, nb, send_row)

    def row_forward(pp, j):
        return pltpu.make_async_remote_copy(
            src_ref=rows.at[pp, j], dst_ref=rows.at[pp, j], send_sem=rows_fwd.at[pp, j], recv_sem=rows_recv.at[pp, j],
            device_id=sibling, device_id_type=MESH)

    @pl.when(bit(row_mask, p))
    def _():
        rows[p, core] = m_own[...]

    @pl.when(keeps)
    def _():
        cols[p, pl.ds(pl.multiple_of(pad * side + tile * core, 16), tile)] = mt_own[...]

    if pad:
        def clear(pp):
            cols[pp, pl.ds(pl.multiple_of(2 * tile * (1 - core), 16), pad)] = jnp.zeros((pad, n), jnp.bfloat16)

        loop(0, nb, clear)
    gram[...] = jnp.zeros_like(gram)

    def col_copy(pp, j):
        place = col_place(pp, core, j)
        return pltpu.make_async_remote_copy(
            src_ref=place, dst_ref=place, send_sem=cols_send.at[pp, j], recv_sem=cols_recv.at[pp, j],
            device_id=chip_at(p, beside, core), device_id_type=MESH)

    def receive(pp):
        for j in range(2):
            @pl.when(~(keeps & (pp == p) & (j == core)))
            def _():
                col_copy(pp, j).wait_recv()

    def hand_on(pp):
        @pl.when(bit(here, pp))
        def _():
            for j in range(2):
                col_copy(pp, j).wait_recv()
                col_copy(pp, j).start()

    def near(i):
        ny = nb // 2
        step = pick(i // 2, [0, 1, ny - 1, 2][:ny] if ny > 2 else [0, 1])
        return 2 * ((p // 2 + step) % ny) + (p + i) % 2

    @pl.when(leads)
    def _():
        loop(0, nb, lambda i: hand_on(near(i)))

    def share_row(pp):
        @pl.when(bit(row_mask, pp))
        def _():
            @pl.when(pp != p)
            def _():
                row_forward(pp, core).wait_recv()

            row_forward(pp, core).start()

    loop(0, nb, share_row)

    give_w.wait_recv()
    load_w.wait()
    from_sibling = diag & (core != side)

    def use(pp):
        @pl.when(~leads)
        def _():
            receive(pp)

        @pl.when(keeps)
        def _():
            for j in range(2):
                part = cols[pp, pl.ds(pl.multiple_of(pad * side + tile * j, 16), tile)]
                rows[pp, j] = part.T

                @pl.when(pp % 2 == side)
                def _():
                    row_forward(pp, j).start()

        @pl.when(~keeps)
        def _():
            for j in range(2):
                @pl.when(from_sibling | (j != core))
                def _():
                    row_forward(pp, j).wait_recv()

        t = jnp.dot(w[...], cols[pp], preferred_element_type=jnp.float32)
        high = t.astype(jnp.bfloat16)
        low = (t - high.astype(jnp.float32)).astype(jnp.bfloat16)
        both = jnp.concatenate([high, low], axis=1)
        g = jnp.dot(rows[pp, 0], both[:tile], preferred_element_type=jnp.float32)
        g += jnp.dot(rows[pp, 1], both[tile:], preferred_element_type=jnp.float32)
        gram[...] += g[:, :n] + g[:, n:]

    def use_all(pp):
        @pl.when(keeps | bit(here, pp))
        def _():
            use(pp)

    loop(0, nb, lambda i: use_all(near(i)))

    bands = n // 16
    row_id = lax.broadcasted_iota(jnp.int32, gram.shape, 0)
    lane_id = lax.broadcasted_iota(jnp.int32, gram.shape, 1)
    kept = jnp.where(row_id % bands == lane_id % bands, gram[...], 0.0) * jnp.where(keeps, 0.5, 1.0)
    red1[place1] = kept.reshape(16, bands, n).sum(axis=1)

    def plane_copy(other):
        return pltpu.make_async_remote_copy(
            src_ref=red1.at[place1], dst_ref=red1.at[place1], send_sem=red1_send.at[other], recv_sem=red1_recv.at[place1],
            device_id=plane_device(other), device_id_type=MESH)

    def plane_wait(other):
        pltpu.make_async_remote_copy(
            src_ref=red1.at[place1], dst_ref=red1.at[other], send_sem=red1_send.at[other], recv_sem=red1_recv.at[other],
            device_id=plane_device(other), device_id_type=MESH).wait_recv()

    loop(1, 2 * nb, lambda i: plane_copy((place1 + i) % (2 * nb)).start())
    give_w.wait_send()
    targets(pair, shard_words, side, p, lambda k, at, to: column_copy(k, at, to).wait_send())

    @pl.when(~keeps)
    def _():
        to_diag.wait_send()

    def sent(pp):
        @pl.when((pp != p) & sends_row(pp))
        def _():
            row_copy(pp).wait_send()

        @pl.when(bit(row_mask, pp))
        def _():
            row_forward(pp, core).wait_send()

        for j in range(2):
            @pl.when(leads & bit(here, pp))
            def _():
                col_copy(pp, j).wait_send()

            @pl.when(keeps & (pp % 2 == side))
            def _():
                row_forward(pp, j).wait_send()

    loop(0, nb, sent)
    loop(1, 2 * nb, lambda i: plane_wait((place1 + i) % (2 * nb)))
    red2[chip] = red1[...].sum(axis=0)

    def line_copy(other):
        return pltpu.make_async_remote_copy(
            src_ref=red2.at[chip], dst_ref=red2.at[chip], send_sem=red2_send.at[other], recv_sem=red2_recv.at[chip],
            device_id=chip_at(p, other, core), device_id_type=MESH)

    def line_wait(other):
        pltpu.make_async_remote_copy(
            src_ref=red2.at[chip], dst_ref=red2.at[other], send_sem=red2_send.at[other], recv_sem=red2_recv.at[other],
            device_id=chip_at(p, other, core), device_id_type=MESH).wait_recv()

    loop(1, 2 * zs, lambda i: line_copy((chip + i) % (2 * zs)).start())
    loop(1, 2 * zs, lambda i: line_wait((chip + i) % (2 * zs)))
    total = red2[...].sum(axis=0)
    fold = jnp.where(
        lax.broadcasted_iota(jnp.int32, (n, 16), 0) // bands == lax.broadcasted_iota(jnp.int32, (n, 16), 1), 1.0, 0.0)
    s = jnp.dot(total, fold, precision=lax.Precision.HIGHEST, preferred_element_type=jnp.float32)
    s_t = lax.dot_general(fold, total, (((0,), (1,)), ((), ())), precision=lax.Precision.HIGHEST,
                          preferred_element_type=jnp.float32)
    out_ref[...] = -(s + s_t)

    loop(1, 2 * nb, lambda i: plane_copy((place1 + i) % (2 * nb)).wait_send())
    loop(1, 2 * zs, lambda i: line_copy((chip + i) % (2 * zs)).wait_send())


def body(nb, pair_matrices, screened):
    states, bands, tile = pair_matrices.shape
    n = states * bands
    flat = pair_matrices.reshape(n, tile)
    window = -(-2 * tile // 128) * 128
    dma = pltpu.SemaphoreType.DMA
    small = pltpu.VMEM((2 * nb, states, n), jnp.float32)
    return pl.pallas_call(
        functools.partial(kernel, nb),
        out_shape=jax.ShapeDtypeStruct((states, states), jnp.float32),
        in_specs=[pl.BlockSpec(memory_space=pl.ANY)] * 2,
        out_specs=pl.BlockSpec(memory_space=pltpu.VMEM),
        scratch_shapes=[
            pltpu.VMEM((n, tile), jnp.bfloat16),
            pltpu.VMEM((tile, n), jnp.bfloat16),
            pltpu.VMEM((2 * tile, window), jnp.bfloat16),
            pltpu.VMEM((nb, 2, n, tile), jnp.bfloat16),
            pltpu.VMEM((nb, window, n), jnp.bfloat16),
            pltpu.VMEM((n, n), jnp.float32),
            small,
            small,
            dma((2,)), dma((2,)), dma((nb + 1,)), dma((nb, 2)), dma((nb, 2)), dma((nb, 2)), dma((nb, 2)), dma((nb, 2)),
            dma((2 * nb,)), dma((2 * nb,)), dma((2 * nb,)), dma((2 * nb,)),
        ],
        compiler_params=pltpu.CompilerParams(collective_id=0, has_side_effects=True, vmem_limit_bytes=40 * 1024 * 1024),
    )(flat, screened)


def solution(mesh):
    placed = (P(None, "band", "grow"), P("grow", "band"))
    return jax.shard_map(functools.partial(body, mesh.shape["band"]), mesh=mesh, in_specs=placed, out_specs=P(), check_vma=False)
```

```python
import functools

import jax
import jax.numpy as jnp
from jax import lax
from jax.experimental import pallas as pl
from jax.experimental.pallas import tpu as pltpu
from jax.sharding import PartitionSpec as P

MESH = pl.DeviceIdType.MESH

SHARES = {
    8: [
        [0, 170, 27, 154, 120, 116, 177, 101],
        [85, 0, 85, 114, 57, 177, 170, 166],
        [228, 170, 0, 170, 198, 85, 106, 89],
        [101, 141, 85, 0, 154, 216, 226, 83],
        [135, 198, 57, 101, 0, 170, 27, 154],
        [139, 78, 170, 39, 85, 0, 85, 114],
        [78, 85, 149, 29, 228, 170, 0, 170],
        [154, 89, 166, 172, 101, 141, 85, 0],
    ],
    4: [[0, 3, 5, 9], [12, 0, 6, 10], [10, 9, 0, 3], [6, 5, 12, 0]],
}


def pick(index, values):
    out = jnp.int32(values[0])
    for i, v in enumerate(values[1:], 1):
        out = jnp.where(index == i, jnp.int32(v), out)
    return out


def bit(mask, i):
    return (mask >> i) & 1 == 1


def loop(lo, hi, act):
    def body(i, carry):
        act(i)
        return carry

    lax.fori_loop(lo, hi, body, 0)


def kernel(nb, m_hbm, w_hbm, out_ref, m_own, mt_own, w, rows, cols, gram, red1, red2,
           load_sem, w_sem, plane_send, rows_recv, rows_fwd, cols_recv, cols_send, column_send,
           red1_send, red1_recv, red2_send, red2_recv):
    share = SHARES[nb]
    zs, pairs = nb, nb // 2
    full = (1 << nb) - 1
    even = sum(1 << i for i in range(0, nb, 2))
    p, q = lax.axis_index("band"), lax.axis_index("grow")
    core, chip = q % 2, q // 2
    pair, side = chip // 2, chip % 2
    diag = pair == p
    tile, n = mt_own.shape
    window = w.shape[1]
    pad = window - 2 * tile
    sibling = (p, q + 1 - 2 * core)

    def chip_at(line, chip_to, core_at):
        return (line, 2 * chip_to + core_at)

    beside = chip + 1 - 2 * side

    load_m = pltpu.make_async_copy(m_hbm, m_own, load_sem.at[0])
    load_m.start()
    own_rows = pl.ds(pl.multiple_of(core * tile, 16), tile)
    far = 4 * tile - window
    load_w = pltpu.make_async_copy(w_hbm.at[:, pl.ds(pl.multiple_of(core * far, 128), window)], w.at[own_rows], load_sem.at[1])
    load_w.start()
    give_w = pltpu.make_async_remote_copy(
        src_ref=w_hbm.at[:, pl.ds(pl.multiple_of((1 - core) * far, 128), window)], dst_ref=w.at[own_rows],
        send_sem=w_sem.at[0], recv_sem=w_sem.at[1], device_id=sibling, device_id_type=MESH)

    barrier = pltpu.get_barrier_semaphore()

    def greet(device):
        pl.semaphore_signal(barrier, inc=1, device_id=device, device_id_type=MESH)

    place1 = 2 * p + core

    def plane_device(i):
        return (i // 2, 2 * chip + i % 2)

    loop(1, 2 * nb, lambda i: greet(plane_device((place1 + i) % (2 * nb))))
    loop(1, 2 * zs, lambda i: greet(chip_at(p, (chip + i) % (2 * zs), core)))

    def words_of(line):
        words = []
        for r in range(2):
            v = [sum(share[r * pairs + i][l] << (nb * i) for i in range(pairs)) for l in range(nb)]
            words.append(pick(line, [x - (x >> 31 << 32) for x in v]))
        return words

    def shared(at, words):
        return (jnp.where(at // pairs == 0, words[0], words[1]) >> (nb * (at % pairs))) & full

    def leader(at, line, c):
        return pick((at + pairs - line % pairs) % pairs, [c, 0] if pairs == 2 else [c, 0, 1 - c, 1])

    def straight(at, line, c):
        ahead = (at + pairs - line % pairs) % pairs
        return ((ahead == 1) & (c == 1)) | ((ahead == pairs - 1) & (c == 0))

    def targets(line, words, c, pp, part, act):
        def one(i):
            at = (line + 2 * nb - 1 - i) % nb
            home = at == line
            goes = jnp.where(home, pp % 2 == 1 - c, bit(shared(at, words), pp))
            to = 2 * at + jnp.where(home, 1 - c, leader(at, line, c))

            both = straight(at, line, c)

            if part == 0:
                @pl.when(goes & ~home & ~both)
                def _():
                    act(0, at, to)
            else:
                @pl.when(goes & (home | both))
                def _():
                    act(0, at, to)

                @pl.when(goes & ~home & both)
                def _():
                    act(1, at, 2 * at + 1 - leader(at, line, c))

        loop(0, nb, one)

    own_words = words_of(p)
    here = jnp.where(~diag, shared(pair, own_words), jnp.where(side == core, 0, jnp.where(side == 0, even, full - even)))
    direct = diag | straight(pair, p, core) | (side == leader(pair, p, core))
    leads = direct & ~diag & ~straight(pair, p, core)
    row_mask = jnp.where(diag, 0, shared(pair, own_words))
    to_lines = jnp.int32(0)
    for l in range(nb):
        m = pick(pair, [share[r][l] for r in range(nb)])
        to_lines |= jnp.where((m >> p) & 1 == 1, 1 << l, 0)
    def greet_sender(pp):
        @pl.when(direct & bit(here, pp))
        def _():
            for j in range(2):
                greet((pp, 2 * (2 * p + core) + j))

    loop(0, nb, greet_sender)
    load_m.wait()
    mt_own[...] = m_own[...].T
    shard_words = words_of(pair)

    def count(i, total):
        at = (pair + i) % nb
        one = bit(shared(at, shard_words), p)
        return total + jnp.where(one, jnp.where(straight(at, pair, side), 2, 1), 0)

    n_columns = lax.fori_loop(1, nb, count, jnp.where(p % 2 == 1 - side, 1, 0))
    pl.semaphore_wait(barrier, 4 * nb - 2 + n_columns)
    give_w.start()

    def col_place(pp, c, j):
        return cols.at[pp, pl.ds(pl.multiple_of(pad * c + tile * j, 16), tile)]

    def column_copy(k, at, to):
        return pltpu.make_async_remote_copy(
            src_ref=mt_own, dst_ref=col_place(p, side, core), send_sem=column_send.at[at, k], recv_sem=cols_recv.at[p, core],
            device_id=chip_at(pair, to, side), device_id_type=MESH)

    def send(k, at, to):
        column_copy(k, at, to).start()

    def sent_column(k, at, to):
        column_copy(k, at, to).wait_send()

    targets(pair, shard_words, side, p, 0, send)
    targets(pair, shard_words, side, p, 0, sent_column)
    targets(pair, shard_words, side, p, 1, send)

    keeps = diag & (core == side)
    to_diag = pltpu.make_async_remote_copy(
        src_ref=mt_own, dst_ref=col_place(p, side, core), send_sem=plane_send.at[nb], recv_sem=cols_recv.at[p, core],
        device_id=(pair, 2 * chip + side), device_id_type=MESH)

    @pl.when(~keeps)
    def _():
        to_diag.start()

    def row_copy(line):
        return pltpu.make_async_remote_copy(
            src_ref=m_own, dst_ref=rows.at[p, core], send_sem=plane_send.at[line], recv_sem=rows_recv.at[p, core],
            device_id=(line, q), device_id_type=MESH)

    def sends_row(line):
        return bit(to_lines, line) & (line != p) & (line != pair)

    def send_row(i):
        line = (p + i) % nb

        @pl.when(sends_row(line))
        def _():
            row_copy(line).start()

    loop(1, nb, send_row)

    def row_forward(pp, j):
        return pltpu.make_async_remote_copy(
            src_ref=rows.at[pp, j], dst_ref=rows.at[pp, j], send_sem=rows_fwd.at[pp, j], recv_sem=rows_recv.at[pp, j],
            device_id=sibling, device_id_type=MESH)

    @pl.when(bit(row_mask, p))
    def _():
        rows[p, core] = m_own[...]

    @pl.when(keeps)
    def _():
        cols[p, pl.ds(pl.multiple_of(pad * side + tile * core, 16), tile)] = mt_own[...]

    if pad:
        def clear(pp):
            cols[pp, pl.ds(pl.multiple_of(2 * tile * (1 - core), 16), pad)] = jnp.zeros((pad, n), jnp.bfloat16)

        loop(0, nb, clear)
    gram[...] = jnp.zeros_like(gram)

    def col_copy(pp, j):
        place = col_place(pp, core, j)
        return pltpu.make_async_remote_copy(
            src_ref=place, dst_ref=place, send_sem=cols_send.at[pp, j], recv_sem=cols_recv.at[pp, j],
            device_id=chip_at(p, beside, core), device_id_type=MESH)

    def receive(pp):
        for j in range(2):
            @pl.when(~(keeps & (pp == p) & (j == core)))
            def _():
                col_copy(pp, j).wait_recv()

    def hand_on(pp):
        @pl.when(bit(here, pp))
        def _():
            for j in range(2):
                col_copy(pp, j).wait_recv()
                col_copy(pp, j).start()

    def near(i):
        ny = nb // 2
        step = pick(i // 2, [0, 1, ny - 1, 2][:ny] if ny > 2 else [0, 1])
        return 2 * ((p // 2 + step) % ny) + (p + i) % 2

    @pl.when(leads)
    def _():
        loop(0, nb, lambda i: hand_on(near(i)))

    def share_row(pp):
        @pl.when(bit(row_mask, pp))
        def _():
            @pl.when(pp != p)
            def _():
                row_forward(pp, core).wait_recv()

            row_forward(pp, core).start()

    loop(0, nb, share_row)

    give_w.wait_recv()
    load_w.wait()
    from_sibling = diag & (core != side)

    def use(pp):
        @pl.when(~leads)
        def _():
            receive(pp)

        @pl.when(keeps)
        def _():
            for j in range(2):
                part = cols[pp, pl.ds(pl.multiple_of(pad * side + tile * j, 16), tile)]
                rows[pp, j] = part.T

                @pl.when(pp % 2 == side)
                def _():
                    row_forward(pp, j).start()

        @pl.when(~keeps)
        def _():
            for j in range(2):
                @pl.when(from_sibling | (j != core))
                def _():
                    row_forward(pp, j).wait_recv()

        t = jnp.dot(w[...], cols[pp], preferred_element_type=jnp.float32)
        high = t.astype(jnp.bfloat16)
        low = (t - high.astype(jnp.float32)).astype(jnp.bfloat16)
        both = jnp.concatenate([high, low], axis=1)
        g = jnp.dot(rows[pp, 0], both[:tile], preferred_element_type=jnp.float32)
        g += jnp.dot(rows[pp, 1], both[tile:], preferred_element_type=jnp.float32)
        gram[...] += g[:, :n] + g[:, n:]

    def use_all(pp):
        @pl.when(keeps | bit(here, pp))
        def _():
            use(pp)

    loop(0, nb, lambda i: use_all(near(i)))

    bands = n // 16
    row_id = lax.broadcasted_iota(jnp.int32, gram.shape, 0)
    lane_id = lax.broadcasted_iota(jnp.int32, gram.shape, 1)
    kept = jnp.where(row_id % bands == lane_id % bands, gram[...], 0.0) * jnp.where(keeps, 0.5, 1.0)
    red1[place1] = kept.reshape(16, bands, n).sum(axis=1)

    def plane_copy(other):
        return pltpu.make_async_remote_copy(
            src_ref=red1.at[place1], dst_ref=red1.at[place1], send_sem=red1_send.at[other], recv_sem=red1_recv.at[place1],
            device_id=plane_device(other), device_id_type=MESH)

    def plane_wait(other):
        pltpu.make_async_remote_copy(
            src_ref=red1.at[place1], dst_ref=red1.at[other], send_sem=red1_send.at[other], recv_sem=red1_recv.at[other],
            device_id=plane_device(other), device_id_type=MESH).wait_recv()

    loop(1, 2 * nb, lambda i: plane_copy((place1 + i) % (2 * nb)).start())
    give_w.wait_send()
    targets(pair, shard_words, side, p, 1, sent_column)

    @pl.when(~keeps)
    def _():
        to_diag.wait_send()

    def sent(pp):
        @pl.when((pp != p) & sends_row(pp))
        def _():
            row_copy(pp).wait_send()

        @pl.when(bit(row_mask, pp))
        def _():
            row_forward(pp, core).wait_send()

        for j in range(2):
            @pl.when(leads & bit(here, pp))
            def _():
                col_copy(pp, j).wait_send()

            @pl.when(keeps & (pp % 2 == side))
            def _():
                row_forward(pp, j).wait_send()

    loop(1, 2 * nb, lambda i: plane_wait((place1 + i) % (2 * nb)))
    red2[chip] = red1[...].sum(axis=0)

    def line_copy(other):
        return pltpu.make_async_remote_copy(
            src_ref=red2.at[chip], dst_ref=red2.at[chip], send_sem=red2_send.at[other], recv_sem=red2_recv.at[chip],
            device_id=chip_at(p, other, core), device_id_type=MESH)

    def line_wait(other):
        pltpu.make_async_remote_copy(
            src_ref=red2.at[chip], dst_ref=red2.at[other], send_sem=red2_send.at[other], recv_sem=red2_recv.at[other],
            device_id=chip_at(p, other, core), device_id_type=MESH).wait_recv()

    loop(1, 2 * zs, lambda i: line_copy((chip + i) % (2 * zs)).start())
    loop(0, nb, sent)
    loop(1, 2 * zs, lambda i: line_wait((chip + i) % (2 * zs)))
    total = red2[...].sum(axis=0)
    fold = jnp.where(
        lax.broadcasted_iota(jnp.int32, (n, 16), 0) // bands == lax.broadcasted_iota(jnp.int32, (n, 16), 1), 1.0, 0.0)
    s = jnp.dot(total, fold, precision=lax.Precision.HIGHEST, preferred_element_type=jnp.float32)
    s_t = lax.dot_general(fold, total, (((0,), (1,)), ((), ())), precision=lax.Precision.HIGHEST,
                          preferred_element_type=jnp.float32)
    out_ref[...] = -(s + s_t)

    loop(1, 2 * nb, lambda i: plane_copy((place1 + i) % (2 * nb)).wait_send())
    loop(1, 2 * zs, lambda i: line_copy((chip + i) % (2 * zs)).wait_send())


def body(nb, pair_matrices, screened):
    states, bands, tile = pair_matrices.shape
    n = states * bands
    flat = pair_matrices.reshape(n, tile)
    window = -(-2 * tile // 128) * 128
    dma = pltpu.SemaphoreType.DMA
    small = pltpu.VMEM((2 * nb, states, n), jnp.float32)
    return pl.pallas_call(
        functools.partial(kernel, nb),
        out_shape=jax.ShapeDtypeStruct((states, states), jnp.float32),
        in_specs=[pl.BlockSpec(memory_space=pl.ANY)] * 2,
        out_specs=pl.BlockSpec(memory_space=pltpu.VMEM),
        scratch_shapes=[
            pltpu.VMEM((n, tile), jnp.bfloat16),
            pltpu.VMEM((tile, n), jnp.bfloat16),
            pltpu.VMEM((2 * tile, window), jnp.bfloat16),
            pltpu.VMEM((nb, 2, n, tile), jnp.bfloat16),
            pltpu.VMEM((nb, window, n), jnp.bfloat16),
            pltpu.VMEM((n, n), jnp.float32),
            small,
            small,
            dma((2,)), dma((2,)), dma((nb + 1,)), dma((nb, 2)), dma((nb, 2)), dma((nb, 2)), dma((nb, 2)), dma((nb, 2)),
            dma((2 * nb,)), dma((2 * nb,)), dma((2 * nb,)), dma((2 * nb,)),
        ],
        compiler_params=pltpu.CompilerParams(collective_id=0, has_side_effects=True, vmem_limit_bytes=40 * 1024 * 1024),
    )(flat, screened)


def solution(mesh):
    placed = (P(None, "band", "grow"), P("grow", "band"))
    return jax.shard_map(functools.partial(body, mesh.shape["band"]), mesh=mesh, in_specs=placed, out_specs=P(), check_vma=False)
```

```python
import functools

import jax
import jax.numpy as jnp
from jax import lax
from jax.experimental import pallas as pl
from jax.experimental.pallas import tpu as pltpu
from jax.sharding import PartitionSpec as P

MESH = pl.DeviceIdType.MESH

SHARES = {
    8: [
        [0, 170, 27, 154, 120, 116, 177, 101],
        [85, 0, 85, 114, 57, 177, 170, 166],
        [228, 170, 0, 170, 198, 85, 106, 89],
        [101, 141, 85, 0, 154, 216, 226, 83],
        [135, 198, 57, 101, 0, 170, 27, 154],
        [139, 78, 170, 39, 85, 0, 85, 114],
        [78, 85, 149, 29, 228, 170, 0, 170],
        [154, 89, 166, 172, 101, 141, 85, 0],
    ],
    4: [[0, 3, 5, 9], [12, 0, 6, 10], [10, 9, 0, 3], [6, 5, 12, 0]],
}


def pick(index, values):
    out = jnp.int32(values[0])
    for i, v in enumerate(values[1:], 1):
        out = jnp.where(index == i, jnp.int32(v), out)
    return out


def bit(mask, i):
    return (mask >> i) & 1 == 1


def loop(lo, hi, act):
    def body(i, carry):
        act(i)
        return carry

    lax.fori_loop(lo, hi, body, 0)


def kernel(nb, m_hbm, w_hbm, out_ref, m_own, mt_own, w, rows, cols, gram, red1, red2,
           load_sem, w_sem, plane_send, rows_recv, rows_fwd, cols_recv, cols_send, column_send,
           red1_send, red1_recv, red2_send, red2_recv):
    share = SHARES[nb]
    zs, pairs = nb, nb // 2
    full = (1 << nb) - 1
    even = sum(1 << i for i in range(0, nb, 2))
    p, q = lax.axis_index("band"), lax.axis_index("grow")
    core, chip = q % 2, q // 2
    pair, side = chip // 2, chip % 2
    diag = pair == p
    tile, n = mt_own.shape
    window = w.shape[1]
    pad = window - 2 * tile
    sibling = (p, q + 1 - 2 * core)

    def chip_at(line, chip_to, core_at):
        return (line, 2 * chip_to + core_at)

    beside = chip + 1 - 2 * side

    load_m = pltpu.make_async_copy(m_hbm, m_own, load_sem.at[0])
    load_m.start()
    own_rows = pl.ds(pl.multiple_of(core * tile, 16), tile)
    far = 4 * tile - window
    load_w = pltpu.make_async_copy(w_hbm.at[:, pl.ds(pl.multiple_of(core * far, 128), window)], w.at[own_rows], load_sem.at[1])
    load_w.start()
    give_w = pltpu.make_async_remote_copy(
        src_ref=w_hbm.at[:, pl.ds(pl.multiple_of((1 - core) * far, 128), window)], dst_ref=w.at[own_rows],
        send_sem=w_sem.at[0], recv_sem=w_sem.at[1], device_id=sibling, device_id_type=MESH)

    barrier = pltpu.get_barrier_semaphore()

    def greet(device):
        pl.semaphore_signal(barrier, inc=1, device_id=device, device_id_type=MESH)

    place1 = 2 * p + core

    def plane_device(i):
        return (i // 2, 2 * chip + i % 2)

    loop(1, 2 * nb, lambda i: greet(plane_device((place1 + i) % (2 * nb))))
    loop(1, 2 * zs, lambda i: greet(chip_at(p, (chip + i) % (2 * zs), core)))

    def words_of(line):
        words = []
        for r in range(2):
            v = [sum(share[r * pairs + i][l] << (nb * i) for i in range(pairs)) for l in range(nb)]
            words.append(pick(line, [x - (x >> 31 << 32) for x in v]))
        return words

    def shared(at, words):
        return (jnp.where(at // pairs == 0, words[0], words[1]) >> (nb * (at % pairs))) & full

    def leader(at, line, c):
        return pick((at + pairs - line % pairs) % pairs, [c, 0] if pairs == 2 else [c, 0, 1 - c, 1])

    def straight(at, line, c):
        ahead = (at + pairs - line % pairs) % pairs
        return ((ahead == 1) & (c == 1)) | ((ahead == pairs - 1) & (c == 0))

    def targets(line, words, c, pp, part, act):
        def one(i):
            at = (line + 2 * nb - 1 - i) % nb
            home = at == line
            goes = jnp.where(home, pp % 2 == 1 - c, bit(shared(at, words), pp))
            to = 2 * at + jnp.where(home, 1 - c, leader(at, line, c))

            both = straight(at, line, c)

            if part == 0:
                @pl.when(goes & ~home & ~both)
                def _():
                    act(0, at, to)
            else:
                @pl.when(goes & (home | both))
                def _():
                    act(0, at, to)

                @pl.when(goes & ~home & both)
                def _():
                    act(1, at, 2 * at + 1 - leader(at, line, c))

        loop(0, nb, one)

    own_words = words_of(p)
    here = jnp.where(~diag, shared(pair, own_words), jnp.where(side == core, 0, jnp.where(side == 0, even, full - even)))
    direct = diag | straight(pair, p, core) | (side == leader(pair, p, core))
    leads = direct & ~diag & ~straight(pair, p, core)
    row_mask = jnp.where(diag, 0, shared(pair, own_words))
    to_lines = jnp.int32(0)
    for l in range(nb):
        m = pick(pair, [share[r][l] for r in range(nb)])
        to_lines |= jnp.where((m >> p) & 1 == 1, 1 << l, 0)
    def greet_sender(pp):
        @pl.when(direct & bit(here, pp))
        def _():
            for j in range(2):
                greet((pp, 2 * (2 * p + core) + j))

    loop(0, nb, greet_sender)
    load_m.wait()
    mt_own[...] = m_own[...].T
    shard_words = words_of(pair)

    def count(i, total):
        at = (pair + i) % nb
        one = bit(shared(at, shard_words), p)
        return total + jnp.where(one, jnp.where(straight(at, pair, side), 2, 1), 0)

    n_columns = lax.fori_loop(1, nb, count, jnp.where(p % 2 == 1 - side, 1, 0))
    pl.semaphore_wait(barrier, 4 * nb - 2 + n_columns)
    give_w.start()

    def col_place(pp, c, j):
        return cols.at[pp, pl.ds(pl.multiple_of(pad * c + tile * j, 16), tile)]

    def column_copy(k, at, to):
        return pltpu.make_async_remote_copy(
            src_ref=mt_own, dst_ref=col_place(p, side, core), send_sem=column_send.at[at, k], recv_sem=cols_recv.at[p, core],
            device_id=chip_at(pair, to, side), device_id_type=MESH)

    def send(k, at, to):
        column_copy(k, at, to).start()

    def sent_column(k, at, to):
        column_copy(k, at, to).wait_send()

    targets(pair, shard_words, side, p, 0, send)
    targets(pair, shard_words, side, p, 0, sent_column)
    targets(pair, shard_words, side, p, 1, send)

    keeps = diag & (core == side)
    to_diag = pltpu.make_async_remote_copy(
        src_ref=mt_own, dst_ref=col_place(p, side, core), send_sem=plane_send.at[nb], recv_sem=cols_recv.at[p, core],
        device_id=(pair, 2 * chip + side), device_id_type=MESH)

    @pl.when(~keeps)
    def _():
        to_diag.start()

    def row_copy(line):
        return pltpu.make_async_remote_copy(
            src_ref=m_own, dst_ref=rows.at[p, core], send_sem=plane_send.at[line], recv_sem=rows_recv.at[p, core],
            device_id=(line, q), device_id_type=MESH)

    def sends_row(line):
        return bit(to_lines, line) & (line != p) & (line != pair)

    def send_row(i):
        line = (p + i) % nb

        @pl.when(sends_row(line))
        def _():
            row_copy(line).start()

    loop(1, nb, send_row)

    def row_forward(pp, j):
        return pltpu.make_async_remote_copy(
            src_ref=rows.at[pp, j], dst_ref=rows.at[pp, j], send_sem=rows_fwd.at[pp, j], recv_sem=rows_recv.at[pp, j],
            device_id=sibling, device_id_type=MESH)

    @pl.when(bit(row_mask, p))
    def _():
        rows[p, core] = m_own[...]

    @pl.when(keeps)
    def _():
        cols[p, pl.ds(pl.multiple_of(pad * side + tile * core, 16), tile)] = mt_own[...]

    if pad:
        def clear(pp):
            cols[pp, pl.ds(pl.multiple_of(2 * tile * (1 - core), 16), pad)] = jnp.zeros((pad, n), jnp.bfloat16)

        loop(0, nb, clear)
    gram[...] = jnp.zeros_like(gram)

    def col_copy(pp, j):
        place = col_place(pp, core, j)
        return pltpu.make_async_remote_copy(
            src_ref=place, dst_ref=place, send_sem=cols_send.at[pp, j], recv_sem=cols_recv.at[pp, j],
            device_id=chip_at(p, beside, core), device_id_type=MESH)

    def receive(pp):
        for j in range(2):
            @pl.when(~(keeps & (pp == p) & (j == core)))
            def _():
                col_copy(pp, j).wait_recv()

    def hand_on(pp):
        @pl.when(bit(here, pp))
        def _():
            for j in range(2):
                col_copy(pp, j).wait_recv()
                col_copy(pp, j).start()

    def near(i):
        ny = nb // 2
        step = pick(i // 2, [0, 1, ny - 1, 2][:ny] if ny > 2 else [0, 1])
        return 2 * ((p // 2 + step) % ny) + (p + i) % 2

    @pl.when(leads)
    def _():
        loop(0, nb, lambda i: hand_on(near(i)))

    def share_row(pp):
        @pl.when(bit(row_mask, pp))
        def _():
            @pl.when(pp != p)
            def _():
                row_forward(pp, core).wait_recv()

            row_forward(pp, core).start()

    loop(0, nb, share_row)

    give_w.wait_recv()
    load_w.wait()
    from_sibling = diag & (core != side)

    def prepare(pp):
        @pl.when(~leads)
        def _():
            receive(pp)

        @pl.when(keeps)
        def _():
            for j in range(2):
                part = cols[pp, pl.ds(pl.multiple_of(pad * side + tile * j, 16), tile)]
                rows[pp, j] = part.T

                @pl.when(pp % 2 == side)
                def _():
                    row_forward(pp, j).start()

        @pl.when(~keeps)
        def _():
            for j in range(2):
                @pl.when(from_sibling | (j != core))
                def _():
                    row_forward(pp, j).wait_recv()

    def multiply(groups):
        right = jnp.concatenate([cols[pp] for pp in groups], axis=1) if len(groups) > 1 else cols[groups[0]]
        t = jnp.dot(w[...], right, preferred_element_type=jnp.float32)
        high = t.astype(jnp.bfloat16)
        low = (t - high.astype(jnp.float32)).astype(jnp.bfloat16)
        for i, pp in enumerate(groups):
            part = slice(i * n, (i + 1) * n)
            both = jnp.concatenate([high[:, part], low[:, part]], axis=1)
            g = jnp.dot(rows[pp, 0], both[:tile], preferred_element_type=jnp.float32)
            g += jnp.dot(rows[pp, 1], both[tile:], preferred_element_type=jnp.float32)
            gram[...] += g[:, :n] + g[:, n:]

    def use_one(i):
        pp = near(i)

        @pl.when(bit(here, pp))
        def _():
            prepare(pp)
            multiply([pp])

    def use_two(i):
        groups = [near(2 * i), near(2 * i + 1)]
        for pp in groups:
            prepare(pp)
        multiply(groups)

    @pl.when(keeps)
    def _():
        loop(0, nb // 2, use_two)

    @pl.when(~keeps)
    def _():
        loop(0, nb, use_one)

    bands = n // 16
    row_id = lax.broadcasted_iota(jnp.int32, gram.shape, 0)
    lane_id = lax.broadcasted_iota(jnp.int32, gram.shape, 1)
    kept = jnp.where(row_id % bands == lane_id % bands, gram[...], 0.0) * jnp.where(keeps, 0.5, 1.0)
    red1[place1] = kept.reshape(16, bands, n).sum(axis=1)

    def plane_copy(other):
        return pltpu.make_async_remote_copy(
            src_ref=red1.at[place1], dst_ref=red1.at[place1], send_sem=red1_send.at[other], recv_sem=red1_recv.at[place1],
            device_id=plane_device(other), device_id_type=MESH)

    def plane_wait(other):
        pltpu.make_async_remote_copy(
            src_ref=red1.at[place1], dst_ref=red1.at[other], send_sem=red1_send.at[other], recv_sem=red1_recv.at[other],
            device_id=plane_device(other), device_id_type=MESH).wait_recv()

    loop(1, 2 * nb, lambda i: plane_copy((place1 + i) % (2 * nb)).start())
    give_w.wait_send()
    targets(pair, shard_words, side, p, 1, sent_column)

    @pl.when(~keeps)
    def _():
        to_diag.wait_send()

    def sent(pp):
        @pl.when((pp != p) & sends_row(pp))
        def _():
            row_copy(pp).wait_send()

        @pl.when(bit(row_mask, pp))
        def _():
            row_forward(pp, core).wait_send()

        for j in range(2):
            @pl.when(leads & bit(here, pp))
            def _():
                col_copy(pp, j).wait_send()

            @pl.when(keeps & (pp % 2 == side))
            def _():
                row_forward(pp, j).wait_send()

    loop(1, 2 * nb, lambda i: plane_wait((place1 + i) % (2 * nb)))
    red2[chip] = red1[...].sum(axis=0)

    def line_copy(other):
        return pltpu.make_async_remote_copy(
            src_ref=red2.at[chip], dst_ref=red2.at[chip], send_sem=red2_send.at[other], recv_sem=red2_recv.at[chip],
            device_id=chip_at(p, other, core), device_id_type=MESH)

    def line_wait(other):
        pltpu.make_async_remote_copy(
            src_ref=red2.at[chip], dst_ref=red2.at[other], send_sem=red2_send.at[other], recv_sem=red2_recv.at[other],
            device_id=chip_at(p, other, core), device_id_type=MESH).wait_recv()

    loop(1, 2 * zs, lambda i: line_copy((chip + i) % (2 * zs)).start())
    loop(0, nb, sent)
    loop(1, 2 * zs, lambda i: line_wait((chip + i) % (2 * zs)))
    total = red2[...].sum(axis=0)
    fold = jnp.where(
        lax.broadcasted_iota(jnp.int32, (n, 16), 0) // bands == lax.broadcasted_iota(jnp.int32, (n, 16), 1), 1.0, 0.0)
    s = jnp.dot(total, fold, precision=lax.Precision.HIGHEST, preferred_element_type=jnp.float32)
    s_t = lax.dot_general(fold, total, (((0,), (1,)), ((), ())), precision=lax.Precision.HIGHEST,
                          preferred_element_type=jnp.float32)
    out_ref[...] = -(s + s_t)

    loop(1, 2 * nb, lambda i: plane_copy((place1 + i) % (2 * nb)).wait_send())
    loop(1, 2 * zs, lambda i: line_copy((chip + i) % (2 * zs)).wait_send())


def body(nb, pair_matrices, screened):
    states, bands, tile = pair_matrices.shape
    n = states * bands
    flat = pair_matrices.reshape(n, tile)
    window = -(-2 * tile // 128) * 128
    dma = pltpu.SemaphoreType.DMA
    small = pltpu.VMEM((2 * nb, states, n), jnp.float32)
    return pl.pallas_call(
        functools.partial(kernel, nb),
        out_shape=jax.ShapeDtypeStruct((states, states), jnp.float32),
        in_specs=[pl.BlockSpec(memory_space=pl.ANY)] * 2,
        out_specs=pl.BlockSpec(memory_space=pltpu.VMEM),
        scratch_shapes=[
            pltpu.VMEM((n, tile), jnp.bfloat16),
            pltpu.VMEM((tile, n), jnp.bfloat16),
            pltpu.VMEM((2 * tile, window), jnp.bfloat16),
            pltpu.VMEM((nb, 2, n, tile), jnp.bfloat16),
            pltpu.VMEM((nb, window, n), jnp.bfloat16),
            pltpu.VMEM((n, n), jnp.float32),
            small,
            small,
            dma((2,)), dma((2,)), dma((nb + 1,)), dma((nb, 2)), dma((nb, 2)), dma((nb, 2)), dma((nb, 2)), dma((nb, 2)),
            dma((2 * nb,)), dma((2 * nb,)), dma((2 * nb,)), dma((2 * nb,)),
        ],
        compiler_params=pltpu.CompilerParams(collective_id=0, has_side_effects=True, vmem_limit_bytes=40 * 1024 * 1024),
    )(flat, screened)


def solution(mesh):
    placed = (P(None, "band", "grow"), P("grow", "band"))
    return jax.shard_map(functools.partial(body, mesh.shape["band"]), mesh=mesh, in_specs=placed, out_specs=P(), check_vma=False)
```

```python
import functools

import jax
import jax.numpy as jnp
from jax import lax
from jax.experimental import pallas as pl
from jax.experimental.pallas import tpu as pltpu
from jax.sharding import PartitionSpec as P

MESH = pl.DeviceIdType.MESH

SHARES = {
    8: [
        [0, 170, 27, 154, 120, 116, 177, 101],
        [85, 0, 85, 114, 57, 177, 170, 166],
        [228, 170, 0, 170, 198, 85, 106, 89],
        [101, 141, 85, 0, 154, 216, 226, 83],
        [135, 198, 57, 101, 0, 170, 27, 154],
        [139, 78, 170, 39, 85, 0, 85, 114],
        [78, 85, 149, 29, 228, 170, 0, 170],
        [154, 89, 166, 172, 101, 141, 85, 0],
    ],
    4: [[0, 3, 5, 9], [12, 0, 6, 10], [10, 9, 0, 3], [6, 5, 12, 0]],
}


def pick(index, values):
    out = jnp.int32(values[0])
    for i, v in enumerate(values[1:], 1):
        out = jnp.where(index == i, jnp.int32(v), out)
    return out


def bit(mask, i):
    return (mask >> i) & 1 == 1


def loop(lo, hi, act):
    def body(i, carry):
        act(i)
        return carry

    lax.fori_loop(lo, hi, body, 0)


def kernel(nb, m_hbm, w_hbm, out_ref, m_own, mt_own, w, rows, cols, gram, red1, red2,
           load_sem, w_sem, plane_send, rows_recv, rows_fwd, cols_recv, cols_send, column_send,
           red1_send, red1_recv, red2_send, red2_recv):
    share = SHARES[nb]
    zs, pairs = nb, nb // 2
    full = (1 << nb) - 1
    even = sum(1 << i for i in range(0, nb, 2))
    p, q = lax.axis_index("band"), lax.axis_index("grow")
    core, chip = q % 2, q // 2
    pair, side = chip // 2, chip % 2
    diag = pair == p
    tile, n = mt_own.shape
    window = w.shape[1]
    pad = window - 2 * tile
    sibling = (p, q + 1 - 2 * core)

    def chip_at(line, chip_to, core_at):
        return (line, 2 * chip_to + core_at)

    beside = chip + 1 - 2 * side

    load_m = pltpu.make_async_copy(m_hbm, m_own, load_sem.at[0])
    load_m.start()
    own_rows = pl.ds(pl.multiple_of(core * tile, 16), tile)
    far = 4 * tile - window
    load_w = pltpu.make_async_copy(w_hbm.at[:, pl.ds(pl.multiple_of(core * far, 128), window)], w.at[own_rows], load_sem.at[1])
    load_w.start()
    give_w = pltpu.make_async_remote_copy(
        src_ref=w_hbm.at[:, pl.ds(pl.multiple_of((1 - core) * far, 128), window)], dst_ref=w.at[own_rows],
        send_sem=w_sem.at[0], recv_sem=w_sem.at[1], device_id=sibling, device_id_type=MESH)

    barrier = pltpu.get_barrier_semaphore()

    def greet(device):
        pl.semaphore_signal(barrier, inc=1, device_id=device, device_id_type=MESH)

    place1 = 2 * p + core

    def plane_device(i):
        return (i // 2, 2 * chip + i % 2)

    loop(1, 2 * nb, lambda i: greet(plane_device((place1 + i) % (2 * nb))))
    loop(1, 2 * zs, lambda i: greet(chip_at(p, (chip + i) % (2 * zs), core)))

    def words_of(line):
        words = []
        for r in range(2):
            v = [sum(share[r * pairs + i][l] << (nb * i) for i in range(pairs)) for l in range(nb)]
            words.append(pick(line, [x - (x >> 31 << 32) for x in v]))
        return words

    def shared(at, words):
        return (jnp.where(at // pairs == 0, words[0], words[1]) >> (nb * (at % pairs))) & full

    def leader(at, line, c):
        return pick((at + pairs - line % pairs) % pairs, [c, 0] if pairs == 2 else [c, 0, 1 - c, 1])

    def straight(at, line, c):
        ahead = (at + pairs - line % pairs) % pairs
        return ((ahead == 1) & (c == 1)) | ((ahead == pairs - 1) & (c == 0))

    def targets(line, words, c, pp, part, act):
        def one(i):
            at = (line + 2 * nb - 1 - i) % nb
            home = at == line
            goes = jnp.where(home, pp % 2 == 1 - c, bit(shared(at, words), pp))
            to = 2 * at + jnp.where(home, 1 - c, leader(at, line, c))

            both = straight(at, line, c)

            if part == 0:
                @pl.when(goes & ~home & ~both)
                def _():
                    act(0, at, to)
            else:
                @pl.when(goes & (home | both))
                def _():
                    act(0, at, to)

                @pl.when(goes & ~home & both)
                def _():
                    act(1, at, 2 * at + 1 - leader(at, line, c))

        loop(0, nb, one)

    own_words = words_of(p)
    here = jnp.where(~diag, shared(pair, own_words), jnp.where(side == core, 0, jnp.where(side == 0, even, full - even)))
    direct = diag | straight(pair, p, core) | (side == leader(pair, p, core))
    leads = direct & ~diag & ~straight(pair, p, core)
    row_mask = jnp.where(diag, 0, shared(pair, own_words))
    to_lines = jnp.int32(0)
    for l in range(nb):
        m = pick(pair, [share[r][l] for r in range(nb)])
        to_lines |= jnp.where((m >> p) & 1 == 1, 1 << l, 0)
    def greet_sender(pp):
        @pl.when(direct & bit(here, pp))
        def _():
            for j in range(2):
                greet((pp, 2 * (2 * p + core) + j))

    loop(0, nb, greet_sender)
    load_m.wait()
    mt_own[...] = m_own[...].T
    shard_words = words_of(pair)

    def count(i, total):
        at = (pair + i) % nb
        one = bit(shared(at, shard_words), p)
        return total + jnp.where(one, jnp.where(straight(at, pair, side), 2, 1), 0)

    n_columns = lax.fori_loop(1, nb, count, jnp.where(p % 2 == 1 - side, 1, 0))
    pl.semaphore_wait(barrier, 4 * nb - 2 + n_columns)
    give_w.start()

    half = tile // 2

    def col_place(pp, c, j, h):
        return cols.at[pp, pl.ds(pl.multiple_of(pad * c + tile * j + half * h, 16), half)]

    def column_copy(k, at, to, h):
        return pltpu.make_async_remote_copy(
            src_ref=mt_own.at[pl.ds(half * h, half)], dst_ref=col_place(p, side, core, h),
            send_sem=column_send.at[at, 2 * k + h], recv_sem=cols_recv.at[p, 2 * core + h],
            device_id=chip_at(pair, to, side), device_id_type=MESH)

    def send(k, at, to):
        for h in range(2):
            column_copy(k, at, to, h).start()

    def sent_column(k, at, to):
        for h in range(2):
            column_copy(k, at, to, h).wait_send()

    targets(pair, shard_words, side, p, 0, send)
    targets(pair, shard_words, side, p, 0, sent_column)
    targets(pair, shard_words, side, p, 1, send)

    keeps = diag & (core == side)
    to_diag = [pltpu.make_async_remote_copy(
        src_ref=mt_own.at[pl.ds(half * h, half)], dst_ref=col_place(p, side, core, h), send_sem=plane_send.at[nb + h],
        recv_sem=cols_recv.at[p, 2 * core + h], device_id=(pair, 2 * chip + side), device_id_type=MESH) for h in range(2)]

    @pl.when(~keeps)
    def _():
        for copy in to_diag:
            copy.start()

    def row_copy(line):
        return pltpu.make_async_remote_copy(
            src_ref=m_own, dst_ref=rows.at[p, core], send_sem=plane_send.at[line], recv_sem=rows_recv.at[p, core],
            device_id=(line, q), device_id_type=MESH)

    def sends_row(line):
        return bit(to_lines, line) & (line != p) & (line != pair)

    def send_row(i):
        line = (p + i) % nb

        @pl.when(sends_row(line))
        def _():
            row_copy(line).start()

    loop(1, nb, send_row)

    def row_forward(pp, j):
        return pltpu.make_async_remote_copy(
            src_ref=rows.at[pp, j], dst_ref=rows.at[pp, j], send_sem=rows_fwd.at[pp, j], recv_sem=rows_recv.at[pp, j],
            device_id=sibling, device_id_type=MESH)

    @pl.when(bit(row_mask, p))
    def _():
        rows[p, core] = m_own[...]

    @pl.when(keeps)
    def _():
        cols[p, pl.ds(pl.multiple_of(pad * side + tile * core, 16), tile)] = mt_own[...]

    if pad:
        def clear(pp):
            cols[pp, pl.ds(pl.multiple_of(2 * tile * (1 - core), 16), pad)] = jnp.zeros((pad, n), jnp.bfloat16)

        loop(0, nb, clear)
    gram[...] = jnp.zeros_like(gram)

    def col_copy(pp, i):
        place = col_place(pp, core, i // 2, i % 2)
        return pltpu.make_async_remote_copy(
            src_ref=place, dst_ref=place, send_sem=cols_send.at[pp, i], recv_sem=cols_recv.at[pp, i],
            device_id=chip_at(p, beside, core), device_id_type=MESH)

    def receive(pp):
        for i in range(4):
            @pl.when(~(keeps & (pp == p) & (i // 2 == core)))
            def _():
                col_copy(pp, i).wait_recv()

    def hand_on(pp):
        @pl.when(bit(here, pp))
        def _():
            for i in range(4):
                col_copy(pp, i).wait_recv()
                col_copy(pp, i).start()

    def near(i):
        ny = nb // 2
        step = pick(i // 2, [0, 1, ny - 1, 2][:ny] if ny > 2 else [0, 1])
        return 2 * ((p // 2 + step) % ny) + (p + i) % 2

    @pl.when(leads)
    def _():
        loop(0, nb, lambda i: hand_on(near(i)))

    def share_row(pp):
        @pl.when(bit(row_mask, pp))
        def _():
            @pl.when(pp != p)
            def _():
                row_forward(pp, core).wait_recv()

            row_forward(pp, core).start()

    loop(0, nb, share_row)

    give_w.wait_recv()
    load_w.wait()
    from_sibling = diag & (core != side)

    def prepare(pp):
        @pl.when(~leads)
        def _():
            receive(pp)

        @pl.when(keeps)
        def _():
            for j in range(2):
                part = cols[pp, pl.ds(pl.multiple_of(pad * side + tile * j, 16), tile)]
                rows[pp, j] = part.T

                @pl.when(pp % 2 == side)
                def _():
                    row_forward(pp, j).start()

        @pl.when(~keeps)
        def _():
            for j in range(2):
                @pl.when(from_sibling | (j != core))
                def _():
                    row_forward(pp, j).wait_recv()

    def multiply(groups):
        right = jnp.concatenate([cols[pp] for pp in groups], axis=1) if len(groups) > 1 else cols[groups[0]]
        t = jnp.dot(w[...], right, preferred_element_type=jnp.float32)
        high = t.astype(jnp.bfloat16)
        low = (t - high.astype(jnp.float32)).astype(jnp.bfloat16)
        for i, pp in enumerate(groups):
            part = slice(i * n, (i + 1) * n)
            both = jnp.concatenate([high[:, part], low[:, part]], axis=1)
            g = jnp.dot(rows[pp, 0], both[:tile], preferred_element_type=jnp.float32)
            g += jnp.dot(rows[pp, 1], both[tile:], preferred_element_type=jnp.float32)
            gram[...] += g[:, :n] + g[:, n:]

    def use_one(i):
        pp = near(i)

        @pl.when(bit(here, pp))
        def _():
            prepare(pp)
            multiply([pp])

    def use_two(i):
        groups = [near(2 * i), near(2 * i + 1)]
        for pp in groups:
            prepare(pp)
        multiply(groups)

    @pl.when(keeps)
    def _():
        loop(0, nb // 2, use_two)

    @pl.when(~keeps)
    def _():
        loop(0, nb, use_one)

    bands = n // 16
    row_id = lax.broadcasted_iota(jnp.int32, gram.shape, 0)
    lane_id = lax.broadcasted_iota(jnp.int32, gram.shape, 1)
    kept = jnp.where(row_id % bands == lane_id % bands, gram[...], 0.0) * jnp.where(keeps, 0.5, 1.0)
    red1[place1] = kept.reshape(16, bands, n).sum(axis=1)

    def plane_copy(other):
        return pltpu.make_async_remote_copy(
            src_ref=red1.at[place1], dst_ref=red1.at[place1], send_sem=red1_send.at[other], recv_sem=red1_recv.at[place1],
            device_id=plane_device(other), device_id_type=MESH)

    def plane_wait(other):
        pltpu.make_async_remote_copy(
            src_ref=red1.at[place1], dst_ref=red1.at[other], send_sem=red1_send.at[other], recv_sem=red1_recv.at[other],
            device_id=plane_device(other), device_id_type=MESH).wait_recv()

    loop(1, 2 * nb, lambda i: plane_copy((place1 + i) % (2 * nb)).start())
    give_w.wait_send()
    targets(pair, shard_words, side, p, 1, sent_column)

    @pl.when(~keeps)
    def _():
        for copy in to_diag:
            copy.wait_send()

    def sent(pp):
        @pl.when((pp != p) & sends_row(pp))
        def _():
            row_copy(pp).wait_send()

        @pl.when(bit(row_mask, pp))
        def _():
            row_forward(pp, core).wait_send()

        for j in range(2):
            @pl.when(leads & bit(here, pp))
            def _():
                for h in range(2):
                    col_copy(pp, 2 * j + h).wait_send()

            @pl.when(keeps & (pp % 2 == side))
            def _():
                row_forward(pp, j).wait_send()

    loop(1, 2 * nb, lambda i: plane_wait((place1 + i) % (2 * nb)))
    red2[chip] = red1[...].sum(axis=0)

    def line_copy(other):
        return pltpu.make_async_remote_copy(
            src_ref=red2.at[chip], dst_ref=red2.at[chip], send_sem=red2_send.at[other], recv_sem=red2_recv.at[chip],
            device_id=chip_at(p, other, core), device_id_type=MESH)

    def line_wait(other):
        pltpu.make_async_remote_copy(
            src_ref=red2.at[chip], dst_ref=red2.at[other], send_sem=red2_send.at[other], recv_sem=red2_recv.at[other],
            device_id=chip_at(p, other, core), device_id_type=MESH).wait_recv()

    loop(1, 2 * zs, lambda i: line_copy((chip + i) % (2 * zs)).start())
    loop(0, nb, sent)
    loop(1, 2 * zs, lambda i: line_wait((chip + i) % (2 * zs)))
    total = red2[...].sum(axis=0)
    fold = jnp.where(
        lax.broadcasted_iota(jnp.int32, (n, 16), 0) // bands == lax.broadcasted_iota(jnp.int32, (n, 16), 1), 1.0, 0.0)
    s = jnp.dot(total, fold, precision=lax.Precision.HIGHEST, preferred_element_type=jnp.float32)
    s_t = lax.dot_general(fold, total, (((0,), (1,)), ((), ())), precision=lax.Precision.HIGHEST,
                          preferred_element_type=jnp.float32)
    out_ref[...] = -(s + s_t)

    loop(1, 2 * nb, lambda i: plane_copy((place1 + i) % (2 * nb)).wait_send())
    loop(1, 2 * zs, lambda i: line_copy((chip + i) % (2 * zs)).wait_send())


def body(nb, pair_matrices, screened):
    states, bands, tile = pair_matrices.shape
    n = states * bands
    flat = pair_matrices.reshape(n, tile)
    window = -(-2 * tile // 128) * 128
    dma = pltpu.SemaphoreType.DMA
    small = pltpu.VMEM((2 * nb, states, n), jnp.float32)
    return pl.pallas_call(
        functools.partial(kernel, nb),
        out_shape=jax.ShapeDtypeStruct((states, states), jnp.float32),
        in_specs=[pl.BlockSpec(memory_space=pl.ANY)] * 2,
        out_specs=pl.BlockSpec(memory_space=pltpu.VMEM),
        scratch_shapes=[
            pltpu.VMEM((n, tile), jnp.bfloat16),
            pltpu.VMEM((tile, n), jnp.bfloat16),
            pltpu.VMEM((2 * tile, window), jnp.bfloat16),
            pltpu.VMEM((nb, 2, n, tile), jnp.bfloat16),
            pltpu.VMEM((nb, window, n), jnp.bfloat16),
            pltpu.VMEM((n, n), jnp.float32),
            small,
            small,
            dma((2,)), dma((2,)), dma((nb + 2,)), dma((nb, 2)), dma((nb, 2)), dma((nb, 4)), dma((nb, 4)), dma((nb, 4)),
            dma((2 * nb,)), dma((2 * nb,)), dma((2 * nb,)), dma((2 * nb,)),
        ],
        compiler_params=pltpu.CompilerParams(collective_id=0, has_side_effects=True, vmem_limit_bytes=40 * 1024 * 1024),
    )(flat, screened)


def solution(mesh):
    placed = (P(None, "band", "grow"), P("grow", "band"))
    return jax.shard_map(functools.partial(body, mesh.shape["band"]), mesh=mesh, in_specs=placed, out_specs=P(), check_vma=False)
```
